32 devices in a mesh: gx: 2 (over core), gy: 4 (over y, x), gz: 4 (over z).
Axes of the slice: x: 2, y: 2, z: 4, core: 2. Of those that a mesh axis runs over, the one named last changes fastest.
Arguments:
- species_field: float32 [48, 2048, 2048], P('gz', 'gx', 'gy')
- x_mode_basis: float32 [2048, 256], P('gx'), may hold values from -0.125 to 0.125
- y_mode_basis: float32 [2048, 256], P('gy'), may hold values from -0.125 to 0.125
Outputs:
- gram_x: float32 [2048, 2048], P(('gx', 'gy'))
- gram_y: float32 [2048, 2048], P('gy', 'gx')
- reduced_core_tensor: float32 [256, 48, 256], P('gx', 'gz', 'gy')
The draws below stay inside these ranges and needn't reach their ends.
All inputs are finite; a program needn't handle non-finite values.
Results may differ from the reference program's by a relative error of at most 0.000092.
Values sent between devices are 32-bit elements; how exact they have to be, the bound alone decides.
A program may use at most 128 MiB of HBM per device.

```python
import math
import jax
import jax.numpy as jnp
from jax import lax

NX = 2048
NY = 2048
SPECIES = 24
PLANES = 2
R = 256
RY = 256


def draw_species_field(key, part):
    key = jax.random.fold_in(key, 11)
    keys = jax.random.split(key, 4)
    slices = SPECIES * PLANES
    spread = math.log(2.0)
    noise_part = jax.random.normal(keys[0], (slices, NX, NY), jnp.float32)
    row_scale_factors = jnp.exp(jax.random.uniform(keys[1], (1, NX, 1), jnp.float32, -spread, spread))
    scale_cols = jnp.exp(jax.random.uniform(keys[2], (1, 1, NY), jnp.float32, -spread, spread))
    scale_slices = jnp.exp(jax.random.uniform(keys[3], (slices, 1, 1), jnp.float32, -spread, spread))
    return noise_part * row_scale_factors * scale_cols * scale_slices


def level_of(stream_key, shape, pieces, smallest, largest):
    level, own = 1.0, jax.random.fold_in(stream_key, 6)
    for dim, parts in pieces:
        steps = jnp.exp(jax.random.uniform(jax.random.fold_in(own, dim), (parts,), jnp.float32, smallest / len(pieces), largest / len(pieces)))
        level = level * jnp.repeat(steps, shape[dim] // parts).reshape([-1 if axis == dim else 1 for axis in range(len(shape))])
    return level


def noise(stream_key, dims, deviation, limit, pieces=(), kind=jnp.bfloat16):
    values = deviation * jax.random.normal(stream_key, dims, jnp.float32)
    if pieces:
        values = values * level_of(stream_key, dims, pieces, -0.22, 0.18)
    return jnp.clip(values, -limit, limit).astype(kind)


def setup_inputs(seed: int = 0) -> dict:
    splits = jax.random.split(jax.random.key(seed), 4)
    return {
        "species_field": draw_species_field(jax.random.fold_in(splits[3], 71), 0),
        "x_mode_basis": noise(splits[1], (NX, R), NX ** -0.5, 0.125, ((0, 2),), jnp.float32),
        "y_mode_basis": noise(splits[2], (NY, RY), NY ** -0.5, 0.125, ((0, 4),), jnp.float32),
    }


def reference(species_field, x_mode_basis, y_mode_basis):
    exact_precision = lax.Precision.HIGHEST
    slices = SPECIES * PLANES
    gram_x = jnp.einsum("sxy,szy->xz", species_field, species_field, precision=exact_precision) / (NY * slices)
    reduced_result = jnp.einsum("xr,sxy->rsy", x_mode_basis, species_field, precision=exact_precision)
    gram_y = jnp.einsum("rsy,rsz->yz", reduced_result, reduced_result, precision=exact_precision) / (R * slices)
    reduced_core_tensor = jnp.einsum("mtl,lw->mtw", reduced_result, y_mode_basis, precision=exact_precision)
    return (gram_x, gram_y, reduced_core_tensor)
```

```python
import functools

import jax
import jax.numpy as jnp
from jax import lax
from jax.experimental import pallas as pl
from jax.experimental.pallas import tpu as pltpu
from jax.sharding import PartitionSpec as P

F32, BF16 = jnp.float32, jnp.bfloat16
LIMIT = 50 * 2**20


def split(x):
    hi = x.astype(BF16)
    return hi, (x - hi.astype(F32)).astype(BF16)


def dot(a, b, dims):
    return lax.dot_general(a, b, (dims, ((), ())), preferred_element_type=F32)


def project_kernel(u_ref, x_ref, keep_ref, send_ref):
    u_hi, u_lo = split(u_ref[...])
    x_hi, x_lo = split(x_ref[0])
    out = dot(
        jnp.concatenate([u_hi, u_hi, u_lo], axis=1),
        jnp.concatenate([x_hi, x_lo, x_hi], axis=0),
        ((1,), (0,)),
    )
    half = keep_ref.shape[1]
    keep_ref[0] = out[:half]
    send_ref[0] = out[half:]


def project(field, basis):
    slices, rows, cols = field.shape
    rank = basis.shape[0]
    out = jax.ShapeDtypeStruct((slices, rank // 2, cols), F32)
    block = pl.BlockSpec((1, rank // 2, cols), lambda s: (s, 0, 0))
    return pl.pallas_call(
        project_kernel,
        grid=(slices,),
        in_specs=[
            pl.BlockSpec((rank, rows), lambda s: (0, 0)),
            pl.BlockSpec((1, rows, cols), lambda s: (s, 0, 0)),
        ],
        out_specs=[block, block],
        out_shape=[out, out],
        compiler_params=pltpu.CompilerParams(vmem_limit_bytes=LIMIT),
        cost_estimate=pl.CostEstimate(
            flops=6 * slices * rows * cols * rank,
            bytes_accessed=4 * slices * cols * (rows + rank),
            transcendentals=0,
        ),
    )(basis, field)


def same_half_kernel(parts, x_ref, out_ref, a_ref, b_ref):
    rows, cols = x_ref.shape[1:]
    b = rows // parts
    wide = out_ref.shape[2]

    @pl.when(pl.program_id(0) == 0)
    def _():
        out_ref[...] = jnp.zeros_like(out_ref)

    hi, lo = split(x_ref[0])
    for n, v in enumerate((hi, hi, lo)):
        a_ref[:, n * cols : (n + 1) * cols] = v
    for n, v in enumerate((hi, lo, hi)):
        b_ref[:rows, n * cols : (n + 1) * cols] = v
        b_ref[rows:, n * cols : (n + 1) * cols] = v[: b_ref.shape[0] - rows]
    for i in range(parts):
        out_ref[i] += dot(a_ref[i * b : (i + 1) * b], b_ref[i * b : i * b + wide], ((1,), (1,)))


def same_half(field, parts):
    slices, rows, cols = field.shape
    b = rows // parts
    wide = b * (parts // 2 + 1)
    return pl.pallas_call(
        functools.partial(same_half_kernel, parts),
        grid=(slices,),
        in_specs=[pl.BlockSpec((1, rows, cols), lambda s: (s, 0, 0))],
        out_specs=pl.BlockSpec((parts, b, wide), lambda s: (0, 0, 0)),
        out_shape=jax.ShapeDtypeStruct((parts, b, wide), F32),
        scratch_shapes=[
            pltpu.VMEM((rows, 3 * cols), BF16),
            pltpu.VMEM((rows + wide - b, 3 * cols), BF16),
        ],
        compiler_params=pltpu.CompilerParams(vmem_limit_bytes=LIMIT),
        cost_estimate=pl.CostEstimate(
            flops=6 * slices * rows * cols * wide,
            bytes_accessed=4 * slices * cols * rows,
            transcendentals=0,
        ),
    )(field)


def cross_kernel(gx_ref, own_ref, other_ref, out_ref, a_ref, b_ref):
    rows, cols = own_ref.shape[1:]

    @pl.when(pl.program_id(0) == 0)
    def _():
        out_ref[...] = jnp.zeros_like(out_ref)

    first = gx_ref[0] == 0
    own, other = own_ref[0], other_ref[0]
    hi, lo = split(jnp.where(first, own, other))
    for n, v in enumerate((hi, hi, lo)):
        a_ref[:, n * cols : (n + 1) * cols] = v
    hi, lo = split(jnp.where(first, other, own))
    for n, v in enumerate((hi, lo, hi)):
        b_ref[:, n * cols : (n + 1) * cols] = v
    b = min(rows, 256)
    for i in range(0, rows, b):
        out_ref[i : i + b] += dot(a_ref[i : i + b], b_ref[...], ((1,), (1,)))


def cross(gx, field, other):
    slices, rows, cols = other.shape
    return pl.pallas_call(
        cross_kernel,
        grid_spec=pltpu.PrefetchScalarGridSpec(
            num_scalar_prefetch=1,
            grid=(slices,),
            in_specs=[
                pl.BlockSpec((1, rows, cols), lambda s, g: (g[0] * slices + s, 0, 0)),
                pl.BlockSpec((1, rows, cols), lambda s, g: (s, 0, 0)),
            ],
            out_specs=pl.BlockSpec((rows, rows), lambda s, g: (0, 0)),
            scratch_shapes=[pltpu.VMEM((rows, 3 * cols), BF16)] * 2,
        ),
        out_shape=jax.ShapeDtypeStruct((rows, rows), F32),
        compiler_params=pltpu.CompilerParams(vmem_limit_bytes=LIMIT),
        cost_estimate=pl.CostEstimate(
            flops=6 * slices * rows * cols * rows,
            bytes_accessed=8 * slices * cols * rows,
            transcendentals=0,
        ),
    )(jnp.reshape(gx, (1,)).astype(jnp.int32), field, other)


def gram_y_kernel(y_ref, out_ref, b_ref):
    parts, depth, cols = y_ref.shape
    wide = out_ref.shape[2]
    i = pl.program_id(0)

    @pl.when(i == 0)
    def _():
        for j in range(b_ref.shape[1] // cols):
            hi, lo = split(y_ref[j % parts])
            b_ref[:, j * cols : (j + 1) * cols] = jnp.concatenate([hi, lo, hi], axis=0)

    hi, lo = split(jnp.transpose(y_ref[i]))
    a = jnp.concatenate([hi, hi, lo], axis=1)
    start = pl.multiple_of(i * cols, cols)
    out_ref[0] = dot(a, b_ref[:, pl.ds(start, wide)], ((1,), (0,)))


def gram_y_terms(y):
    parts, depth, cols = y.shape
    wide = cols * (parts // 2 + 1)
    return pl.pallas_call(
        gram_y_kernel,
        grid=(parts,),
        in_specs=[pl.BlockSpec((parts, depth, cols), lambda i: (0, 0, 0))],
        out_specs=pl.BlockSpec((1, cols, wide), lambda i: (i, 0, 0)),
        out_shape=jax.ShapeDtypeStruct((parts, cols, wide), F32),
        scratch_shapes=[pltpu.VMEM((3 * depth, parts * cols + wide - cols), BF16)],
        compiler_params=pltpu.CompilerParams(vmem_limit_bytes=LIMIT),
        cost_estimate=pl.CostEstimate(
            flops=6 * parts * depth * cols * wide,
            bytes_accessed=4 * parts * cols * (wide + depth),
            transcendentals=0,
        ),
    )(y)


def swap(x, axis_name):
    return lax.ppermute(x, axis_name, [(0, 1), (1, 0)])


def unroll(piece, gy, parts):
    b = piece.shape[1] // (parts // 2 + 1)
    blocks = [piece[:, k * b : (k + 1) * b] for k in range(parts // 2 + 1)]
    mirrored = []
    for k in range(parts // 2 + 1, parts):
        step = parts - k
        perm = [(i, (i + step) % parts) for i in range(parts)]
        mirrored.append(lax.ppermute(blocks[step], "gy", perm).T)
    full = jnp.concatenate(blocks + mirrored, axis=1)
    twice = jnp.concatenate([full, full], axis=1)
    return lax.dynamic_slice_in_dim(twice, ((parts - gy) % parts) * b, parts * b, axis=1)


def per_device(field, x_basis, y_basis):
    gx, gy = lax.axis_index("gx"), lax.axis_index("gy")
    parts, planes = lax.axis_size("gy"), lax.axis_size("gz")
    slices, rows, cols = field.shape
    rank = x_basis.shape[1]
    total_y, total_slices = cols * parts, slices * planes
    half = slices // 2

    basis = jnp.roll(x_basis.T, -gx * (rank // 2), axis=0)
    keep, send = project(field, basis)
    reduced = keep + swap(send, "gx")

    other = swap(lax.dynamic_slice_in_dim(field, (1 - gx) * half, half, axis=0), "gx")

    share = slices * (rank // 2) // parts
    y_rows = lax.all_to_all(reduced.reshape(parts, share, cols), "gy", 0, 0, tiled=True)
    y_basis_all = lax.all_gather(y_basis, "gy", axis=0)

    same = same_half(field, parts)
    across = cross(gx, field, other)

    b = rows // parts
    across = across.reshape(parts, b, 2, rows // 2)
    mine = lax.dynamic_index_in_dim(across, gx, axis=2, keepdims=False)
    theirs = swap(lax.dynamic_index_in_dim(across, 1 - gx, axis=2, keepdims=False), "gx")
    packed = jnp.concatenate([same, mine + theirs], axis=2)
    packed = lax.psum_scatter(packed, "gy", scatter_dimension=0, tiled=True)[0]
    packed = lax.psum(packed, "gz") / (total_y * total_slices)

    terms = gram_y_terms(y_rows)
    wide = terms.shape[2]
    terms = terms.reshape(parts, 2, cols // 2, wide)
    mine = lax.dynamic_index_in_dim(terms, gx, axis=1, keepdims=False)
    theirs = swap(lax.dynamic_index_in_dim(terms, 1 - gx, axis=1, keepdims=False), "gx")
    part_y = lax.psum_scatter(mine + theirs, "gy", scatter_dimension=0, tiled=True)[0]
    part_y = lax.psum(part_y, "gz") / (rank * total_slices)

    core = jnp.einsum("gkl,glq->kq", y_rows, y_basis_all, precision=lax.Precision.HIGH)
    q = core.shape[1]
    core = lax.all_to_all(
        core.reshape(share, parts, q // parts).transpose(1, 0, 2), "gy", 0, 0, tiled=True
    )
    core = core.reshape(slices, rank // 2, q // parts).transpose(1, 0, 2)

    wide_x = same.shape[2]
    diagonal = unroll(packed[:, :wide_x], gy, parts)
    mine = packed[:, wide_x:]
    theirs = swap(mine, "gx")
    strip = jnp.where(
        gx == 0,
        jnp.concatenate([mine, theirs], axis=1),
        jnp.concatenate([theirs, mine], axis=1),
    )
    columns = lax.all_to_all(
        strip.reshape(b, parts, b).transpose(1, 2, 0), "gy", 0, 0, tiled=True
    )
    columns = columns.transpose(1, 0, 2).reshape(b, rows)
    gram_x = jnp.where(
        gx == 0,
        jnp.concatenate([diagonal, strip], axis=1),
        jnp.concatenate([columns, diagonal], axis=1),
    )

    theirs = swap(part_y, "gx")
    both = jnp.where(
        gx == 0,
        jnp.concatenate([part_y, theirs], axis=0),
        jnp.concatenate([theirs, part_y], axis=0),
    )
    both = unroll(both, gy, parts)
    gram_y = lax.dynamic_slice_in_dim(both, gx * (total_y // 2), total_y // 2, axis=1)
    return (gram_x, gram_y, core)


def solution(mesh):
    in_specs = (P("gz", "gx", "gy"), P("gx", None), P("gy", None))
    out_specs = (P(("gx", "gy"), None), P("gy", "gx"), P("gx", "gz", "gy"))
    return jax.shard_map(
        per_device, mesh=mesh, in_specs=in_specs, out_specs=out_specs, check_vma=False
    )
```

```python
import functools

import jax
import jax.numpy as jnp
from jax import lax
from jax.experimental import pallas as pl
from jax.experimental.pallas import tpu as pltpu
from jax.sharding import PartitionSpec as P

F32, BF16 = jnp.float32, jnp.bfloat16
LIMIT = 50 * 2**20
MESH = pl.DeviceIdType.MESH


def split(x):
    hi = x.astype(BF16)
    return hi, (x - hi.astype(F32)).astype(BF16)


def dot(a, b, dims):
    return lax.dot_general(a, b, (dims, ((), ())), preferred_element_type=F32)


def project_kernel(u_ref, x_ref, keep_ref, send_ref):
    u_hi, u_lo = split(u_ref[...])
    x_hi, x_lo = split(x_ref[0])
    out = dot(
        jnp.concatenate([u_hi, u_hi, u_lo], axis=1),
        jnp.concatenate([x_hi, x_lo, x_hi], axis=0),
        ((1,), (0,)),
    )
    half = keep_ref.shape[1]
    keep_ref[0] = out[:half]
    send_ref[0] = out[half:]


def project(field, basis):
    slices, rows, cols = field.shape
    rank = basis.shape[0]
    out = jax.ShapeDtypeStruct((slices, rank // 2, cols), F32)
    block = pl.BlockSpec((1, rank // 2, cols), lambda s: (s, 0, 0))
    return pl.pallas_call(
        project_kernel,
        grid=(slices,),
        in_specs=[
            pl.BlockSpec((rank, rows), lambda s: (0, 0)),
            pl.BlockSpec((1, rows, cols), lambda s: (s, 0, 0)),
        ],
        out_specs=[block, block],
        out_shape=[out, out],
        compiler_params=pltpu.CompilerParams(vmem_limit_bytes=LIMIT),
        cost_estimate=pl.CostEstimate(
            flops=6 * slices * rows * cols * rank,
            bytes_accessed=4 * slices * cols * (rows + rank),
            transcendentals=0,
        ),
    )(basis, field)


def same_half_kernel(parts, x_ref, field_ref, out_ref, other_ref, a_ref, b_ref, send_sem, recv_sem):
    rows, cols = x_ref.shape[1:]
    b = rows // parts
    wide = out_ref.shape[2]
    half = other_ref.shape[0]
    gx = lax.axis_index("gx")
    step = pl.program_id(0)
    copy = pltpu.make_async_remote_copy(
        src_ref=field_ref.at[pl.ds((1 - gx) * half, half)],
        dst_ref=other_ref,
        send_sem=send_sem,
        recv_sem=recv_sem,
        device_id={"gx": 1 - gx},
        device_id_type=MESH,
    )

    @pl.when(step == 0)
    def _():
        barrier = pltpu.get_barrier_semaphore()
        pl.semaphore_signal(barrier, inc=1, device_id={"gx": 1 - gx}, device_id_type=MESH)
        pl.semaphore_wait(barrier, 1)
        copy.start()
        out_ref[...] = jnp.zeros_like(out_ref)

    hi, lo = split(x_ref[0])
    for n, v in enumerate((hi, hi, lo)):
        a_ref[:, n * cols : (n + 1) * cols] = v
    for n, v in enumerate((hi, lo, hi)):
        b_ref[:rows, n * cols : (n + 1) * cols] = v
        b_ref[rows:, n * cols : (n + 1) * cols] = v[: b_ref.shape[0] - rows]
    for i in range(parts):
        out_ref[i] += dot(a_ref[i * b : (i + 1) * b], b_ref[i * b : i * b + wide], ((1,), (1,)))

    @pl.when(step == pl.num_programs(0) - 1)
    def _():
        copy.wait()


def same_half(field, parts):
    slices, rows, cols = field.shape
    b = rows // parts
    wide = b * (parts // 2 + 1)
    return pl.pallas_call(
        functools.partial(same_half_kernel, parts),
        grid=(slices,),
        in_specs=[
            pl.BlockSpec((1, rows, cols), lambda s: (s, 0, 0)),
            pl.BlockSpec(memory_space=pl.ANY),
        ],
        out_specs=[
            pl.BlockSpec((parts, b, wide), lambda s: (0, 0, 0)),
            pl.BlockSpec(memory_space=pl.ANY),
        ],
        out_shape=[
            jax.ShapeDtypeStruct((parts, b, wide), F32),
            jax.ShapeDtypeStruct((slices // 2, rows, cols), F32),
        ],
        scratch_shapes=[
            pltpu.VMEM((rows, 3 * cols), BF16),
            pltpu.VMEM((rows + wide - b, 3 * cols), BF16),
            pltpu.SemaphoreType.DMA,
            pltpu.SemaphoreType.DMA,
        ],
        compiler_params=pltpu.CompilerParams(
            collective_id=2, has_side_effects=True, vmem_limit_bytes=LIMIT
        ),
        cost_estimate=pl.CostEstimate(
            flops=6 * slices * rows * cols * wide,
            bytes_accessed=4 * slices * cols * rows,
            transcendentals=0,
        ),
    )(field, field)


def cross_kernel(gx_ref, own_ref, other_ref, keep_ref, send_ref, a_ref, b_ref):
    rows, cols = own_ref.shape[1:]

    @pl.when(pl.program_id(0) == 0)
    def _():
        keep_ref[...] = jnp.zeros_like(keep_ref)
        send_ref[...] = jnp.zeros_like(send_ref)

    first = gx_ref[0] == 0
    own, other = own_ref[0], other_ref[0]
    hi, lo = split(jnp.where(first, own, other))
    for n, v in enumerate((hi, hi, lo)):
        a_ref[:, n * cols : (n + 1) * cols] = v
    hi, lo = split(jnp.where(first, other, own))
    for n, v in enumerate((hi, lo, hi)):
        b_ref[:, n * cols : (n + 1) * cols] = v
    parts, b, half = keep_ref.shape
    for ref, g in ((keep_ref, gx_ref[0]), (send_ref, 1 - gx_ref[0])):
        right = b_ref[pl.ds(pl.multiple_of(g * half, half), half)]
        for i in range(parts):
            ref[i] += dot(a_ref[i * b : (i + 1) * b], right, ((1,), (1,)))


def cross(gx, field, other, parts):
    slices, rows, cols = other.shape
    shape = (parts, rows // parts, rows // 2)
    return pl.pallas_call(
        cross_kernel,
        grid_spec=pltpu.PrefetchScalarGridSpec(
            num_scalar_prefetch=1,
            grid=(slices,),
            in_specs=[
                pl.BlockSpec((1, rows, cols), lambda s, g: (g[0] * slices + s, 0, 0)),
                pl.BlockSpec((1, rows, cols), lambda s, g: (s, 0, 0)),
            ],
            out_specs=[pl.BlockSpec(shape, lambda s, g: (0, 0, 0))] * 2,
            scratch_shapes=[pltpu.VMEM((rows, 3 * cols), BF16)] * 2,
        ),
        out_shape=[jax.ShapeDtypeStruct(shape, F32)] * 2,
        compiler_params=pltpu.CompilerParams(vmem_limit_bytes=LIMIT),
        cost_estimate=pl.CostEstimate(
            flops=6 * slices * rows * cols * rows,
            bytes_accessed=8 * slices * cols * rows,
            transcendentals=0,
        ),
    )(jnp.reshape(gx, (1,)).astype(jnp.int32), field, other)


def gram_y_kernel(gx_ref, y_ref, keep_ref, send_ref, b_ref):
    parts, depth, cols = y_ref.shape
    wide = keep_ref.shape[2]
    i = pl.program_id(0)

    @pl.when(i == 0)
    def _():
        for j in range(b_ref.shape[1] // cols):
            hi, lo = split(y_ref[j % parts])
            b_ref[:, j * cols : (j + 1) * cols] = jnp.concatenate([hi, lo, hi], axis=0)

    hi, lo = split(jnp.transpose(y_ref[i]))
    a = jnp.concatenate([hi, hi, lo], axis=1)
    start = pl.multiple_of(i * cols, cols)
    out = dot(a, b_ref[:, pl.ds(start, wide)], ((1,), (0,)))

    @pl.when(gx_ref[0] == 0)
    def _():
        keep_ref[0] = out[: cols // 2]
        send_ref[0] = out[cols // 2 :]

    @pl.when(gx_ref[0] == 1)
    def _():
        keep_ref[0] = out[cols // 2 :]
        send_ref[0] = out[: cols // 2]


def gram_y_terms(gx, y):
    parts, depth, cols = y.shape
    wide = cols * (parts // 2 + 1)
    return pl.pallas_call(
        gram_y_kernel,
        grid_spec=pltpu.PrefetchScalarGridSpec(
            num_scalar_prefetch=1,
            grid=(parts,),
            in_specs=[pl.BlockSpec((parts, depth, cols), lambda i, g: (0, 0, 0))],
            out_specs=[pl.BlockSpec((1, cols // 2, wide), lambda i, g: (i, 0, 0))] * 2,
            scratch_shapes=[pltpu.VMEM((3 * depth, parts * cols + wide - cols), BF16)],
        ),
        out_shape=[jax.ShapeDtypeStruct((parts, cols // 2, wide), F32)] * 2,
        compiler_params=pltpu.CompilerParams(vmem_limit_bytes=LIMIT),
        cost_estimate=pl.CostEstimate(
            flops=6 * parts * depth * cols * wide,
            bytes_accessed=4 * parts * cols * (wide + depth),
            transcendentals=0,
        ),
    )(jnp.reshape(gx, (1,)).astype(jnp.int32), y)


def spread(m, bits):
    return sum(((m >> (len(bits) - 1 - j)) & 1) << k for j, k in enumerate(bits))


def reduce_kernel(parts, planes, pieces, *refs):
    n = len(pieces)
    given = [a for a in range(n) if pieces[a][2]]
    g = len(given)
    ins, sends, outs, refs = refs[:n], refs[n : n + g], refs[n + g : 2 * n + g], refs[2 * n + g :]
    sends, partner = dict(zip(given, sends)), dict(zip(given, refs[:g]))
    refs = refs[g:]
    nbits = parts.bit_length() - 1
    steps = [refs[t * n : (t + 1) * n] for t in range(nbits)]
    z_in, z_mid, z_out = (refs[t * n : (t + 1) * n] for t in range(nbits, nbits + 3))
    send_sem, recv_sem = refs[(nbits + 3) * n :]
    gx, gy, gz = lax.axis_index("gx"), lax.axis_index("gy"), lax.axis_index("gz")
    terms = [partner.get(a, ins[a]) for a in range(n)]
    bit = [(gy // 2**k) % 2 for k in range(nbits)]
    side = gz // (planes // 2)
    depth = gz + side * (planes - 1 - 2 * gz)
    inward, outward = gz + 1 - 2 * side, gz - 1 + 2 * side
    middle = planes // 2 - 1

    chunks = []
    for a, (h, count, _) in enumerate(pieces):
        for c in range(count):
            rows = pl.ds(c * (h // count), h // count)
            order = list(range(nbits)) if c % 2 else list(range(nbits))[::-1]
            chunks.append((a, rows, order))

    barrier = pltpu.get_barrier_semaphore()
    for k in range(nbits):
        pl.semaphore_signal(
            barrier, inc=1, device_id={"gy": gy + (1 - 2 * bit[k]) * 2**k}, device_id_type=MESH
        )
    pl.semaphore_signal(barrier, inc=1, device_id={"gx": 1 - gx}, device_id_type=MESH)
    pl.semaphore_signal(barrier, inc=1, device_id={"gz": inward}, device_id_type=MESH)

    @pl.when(depth > 0)
    def _():
        pl.semaphore_signal(barrier, inc=1, device_id={"gz": outward}, device_id_type=MESH)

    pl.semaphore_wait(barrier, nbits + 2 + (depth + planes - 1) // planes)

    def across(c):
        a, rows, order = chunks[c]
        slot = parts // 2 + nbits + 2
        return pltpu.make_async_remote_copy(
            src_ref=sends[a].at[:, rows],
            dst_ref=partner[a].at[:, rows],
            send_sem=send_sem.at[c, slot],
            recv_sem=recv_sem.at[c, slot],
            device_id={"gx": 1 - gx},
            device_id_type=MESH,
        )

    def first(c):
        a, rows, order = chunks[c]
        if a in given:
            across(c).wait_recv()
            for m in range(parts):
                partner[a][m, rows] += ins[a][m, rows]
        for copy in halving(0, c):
            copy.start()

    def halving(t, c):
        a, rows, order = chunks[c]
        k = order[t]
        to = {"gy": gy + (1 - 2 * bit[k]) * 2**k}
        left = 2 ** (nbits - 1 - t)
        if t == 0:
            base = (1 - bit[k]) * 2**k
            return [
                pltpu.make_async_remote_copy(
                    src_ref=terms[a].at[base + spread(m, order[1:]), rows],
                    dst_ref=steps[0][a].at[m, rows],
                    send_sem=send_sem.at[c, m],
                    recv_sem=recv_sem.at[c, m],
                    device_id=to,
                    device_id_type=MESH,
                )
                for m in range(left)
            ]
        slot = parts // 2 + t - 1
        return [
            pltpu.make_async_remote_copy(
                src_ref=steps[t - 1][a].at[pl.ds((1 - bit[k]) * left, left), rows],
                dst_ref=steps[t][a].at[:, rows],
                send_sem=send_sem.at[c, slot],
                recv_sem=recv_sem.at[c, slot],
                device_id=to,
                device_id_type=MESH,
            )
        ]

    def along_z(c, kind):
        a, rows, order = chunks[c]
        slot = parts // 2 + nbits - 1 + kind
        total = steps[nbits - 1][a].at[0, rows]
        src = (total, total, z_out[a].at[rows])[kind]
        dst = (z_in, z_mid, z_out)[kind][a].at[rows]
        return pltpu.make_async_remote_copy(
            src_ref=src,
            dst_ref=dst,
            send_sem=send_sem.at[c, slot],
            recv_sem=recv_sem.at[c, slot],
            device_id={"gz": outward if kind == 2 else inward},
            device_id_type=MESH,
        )

    def stage(t, c):
        a, rows, order = chunks[c]
        if t < nbits:
            for copy in halving(t, c):
                copy.wait_recv()
            k = order[t]
            left = 2 ** (nbits - 1 - t)
            for m in range(left):
                if t == 0:
                    own = terms[a][bit[k] * 2**k + spread(m, order[1:]), rows]
                else:
                    own = steps[t - 1][a][bit[k] * left + m, rows]
                steps[t][a][m, rows] += own
            if t + 1 < nbits:
                for copy in halving(t + 1, c):
                    copy.start()
            else:
                @pl.when((depth == 0) if middle > 0 else (depth > planes))
                def _():
                    along_z(c, 0).start()

        elif t == nbits:
            @pl.when(depth > 0)
            def _():
                along_z(c, 0).wait_recv()
                steps[nbits - 1][a][0, rows] += z_in[a][rows]

            @pl.when(depth == middle)
            def _():
                along_z(c, 1).start()

            if middle > 1:
                @pl.when((depth > 0) & (depth < middle))
                def _():
                    along_z(c, 0).start()

        else:
            @pl.when(depth == middle)
            def _():
                along_z(c, 1).wait_recv()
                z_out[a][rows] = steps[nbits - 1][a][0, rows] + z_mid[a][rows]

            @pl.when(depth < middle)
            def _():
                along_z(c, 2).wait_recv()

            @pl.when(depth > 0)
            def _():
                along_z(c, 2).start()

            outs[a][rows] = z_out[a][rows]

    for c in range(len(chunks)):
        if chunks[c][0] in given:
            across(c).start()
    stages, ahead = nbits + 2, 3
    for c in range(ahead):
        first(c)
    for tick in range(len(chunks) + stages - 1):
        if tick + ahead < len(chunks):
            first(tick + ahead)
        for t in range(stages):
            if 0 <= tick - t < len(chunks):
                stage(t, tick - t)
    for c in range(len(chunks)):
        if chunks[c][0] in given:
            across(c).wait_send()
        for t in range(nbits):
            for copy in halving(t, c):
                copy.wait_send()

        @pl.when(depth < middle)
        def _():
            along_z(c, 0).wait_send()

        @pl.when(depth == middle)
        def _():
            along_z(c, 1).wait_send()

        @pl.when(depth > 0)
        def _():
            along_z(c, 2).wait_send()


def reduce_all(arrays, sends, parts, planes, counts, collective_id):
    pieces = [(x.shape[1], n, y is not None) for x, y, n in zip(arrays, sends, counts)]
    sends = [y for y in sends if y is not None]
    size = sum(x.size for x in arrays)
    nbits = parts.bit_length() - 1
    slots = parts // 2 + nbits + 3
    sems = pltpu.SemaphoreType.DMA((sum(counts), slots))
    vmem = pl.BlockSpec(memory_space=pltpu.VMEM)
    return pl.pallas_call(
        functools.partial(reduce_kernel, parts, planes, pieces),
        in_specs=[vmem] * len(arrays) + [pl.BlockSpec(memory_space=pl.ANY)] * len(sends),
        out_specs=[vmem] * len(arrays),
        out_shape=[jax.ShapeDtypeStruct(x.shape[1:], F32) for x in arrays],
        scratch_shapes=[pltpu.VMEM(x.shape, F32) for x in sends]
        + [
            pltpu.VMEM((parts // 2 ** (t + 1),) + x.shape[1:], F32) for t in range(nbits) for x in arrays
        ]
        + [pltpu.VMEM(x.shape[1:], F32) for x in arrays] * 3
        + [sems, sems],
        compiler_params=pltpu.CompilerParams(
            collective_id=collective_id, has_side_effects=True, vmem_limit_bytes=58 * 2**20
        ),
        cost_estimate=pl.CostEstimate(
            flops=2 * size, bytes_accessed=4 * size, transcendentals=0
        ),
    )(*arrays, *sends)


def swap(x, axis_name):
    return lax.ppermute(x, axis_name, [(0, 1), (1, 0)])


def mirror(block, step, parts):
    perm = [(i, (i + step) % parts) for i in range(parts)]
    return lax.ppermute(block, "gy", perm).T


def unroll(piece, gy, parts):
    b = piece.shape[1] // (parts // 2 + 1)
    blocks = [piece[:, k * b : (k + 1) * b] for k in range(parts // 2 + 1)]
    mirrored = [mirror(blocks[step], step, parts) for step in range(parts // 2 - 1, 0, -1)]
    return pick(blocks + mirrored, [(j + parts - gy) % parts for j in range(parts)])


def pick(blocks, places):
    stack = jnp.stack(blocks)
    return jnp.concatenate(
        [lax.dynamic_index_in_dim(stack, k, axis=0, keepdims=False) for k in places], axis=1
    )


def per_device(field, x_basis, y_basis):
    gx, gy = lax.axis_index("gx"), lax.axis_index("gy")
    parts, planes = lax.axis_size("gy"), lax.axis_size("gz")
    slices, rows, cols = field.shape
    rank = x_basis.shape[1]
    total_y, total_slices = cols * parts, slices * planes
    half = slices // 2

    basis = jnp.roll(x_basis.T, -gx * (rank // 2), axis=0)
    keep, send = project(field, basis)
    reduced = keep + swap(send, "gx")

    share = slices * (rank // 2) // parts
    y_basis_all = lax.all_gather(y_basis, "gy", axis=0)

    reduced, field = lax.optimization_barrier((reduced, field))
    y_rows = lax.all_to_all(reduced.reshape(parts, share, cols), "gy", 0, 0, tiled=True)
    same, other = same_half(field, parts)
    keep_x, send_x = cross(gx, field, other, parts)
    y_rows, same = lax.optimization_barrier((y_rows, same))
    keep_y, send_y = gram_y_terms(gx, y_rows)

    same, across, part_y = reduce_all(
        (same, keep_x, keep_y), (None, send_x, send_y), parts, planes, (4, 4, 4), 1
    )
    same, across = same / (total_y * total_slices), across / (total_y * total_slices)
    part_y = part_y / (rank * total_slices)

    core = jnp.einsum("gkl,glq->kq", y_rows, y_basis_all, precision=lax.Precision.HIGH)
    q = core.shape[1]
    core = lax.all_to_all(
        core.reshape(share, parts, q // parts).transpose(1, 0, 2), "gy", 0, 0, tiled=True
    )
    core = core.reshape(slices, rank // 2, q // parts).transpose(1, 0, 2)

    b = rows // parts
    diagonal = unroll(same, gy, parts)
    mine = across
    theirs = swap(mine, "gx")
    strip = jnp.where(
        gx == 0,
        jnp.concatenate([mine, theirs], axis=1),
        jnp.concatenate([theirs, mine], axis=1),
    )
    columns = lax.all_to_all(
        strip.reshape(b, parts, b).transpose(1, 2, 0), "gy", 0, 0, tiled=True
    )
    columns = columns.transpose(1, 0, 2).reshape(b, rows)
    gram_x = jnp.where(
        gx == 0,
        jnp.concatenate([diagonal, strip], axis=1),
        jnp.concatenate([columns, diagonal], axis=1),
    )

    blocks = [part_y[:, k * cols : (k + 1) * cols] for k in range(parts // 2 + 1)]
    mirrored = [mirror(blocks[step], step, parts) for step in range(parts // 2 - 1, 0, -1)]
    theirs = swap((part_y, mirrored), "gx")
    whole = jnp.where(
        gx == 0,
        jnp.concatenate([part_y, theirs[0]], axis=0),
        jnp.concatenate([theirs[0], part_y], axis=0),
    )
    blocks = [whole[:, k * cols : (k + 1) * cols] for k in range(parts // 2 + 1)]
    for own, got in zip(mirrored, theirs[1]):
        blocks.append(
            jnp.where(
                gx == 0,
                jnp.concatenate([own, got], axis=1),
                jnp.concatenate([got, own], axis=1),
            )
        )
    first = gx * (parts // 2) + parts - gy
    gram_y = pick(blocks, [(first + j) % parts for j in range(parts // 2)])
    return (gram_x, gram_y, core)


def solution(mesh):
    in_specs = (P("gz", "gx", "gy"), P("gx", None), P("gy", None))
    out_specs = (P(("gx", "gy"), None), P("gy", "gx"), P("gx", "gz", "gy"))
    return jax.shard_map(
        per_device, mesh=mesh, in_specs=in_specs, out_specs=out_specs, check_vma=False
    )
```

```python
import functools

import jax
import jax.numpy as jnp
from jax import lax
from jax.experimental import pallas as pl
from jax.experimental.pallas import tpu as pltpu
from jax.sharding import PartitionSpec as P

F32, BF16 = jnp.float32, jnp.bfloat16
LIMIT = 50 * 2**20
MESH = pl.DeviceIdType.MESH


def split(x):
    hi = x.astype(BF16)
    return hi, (x - hi.astype(F32)).astype(BF16)


def dot(a, b, dims):
    return lax.dot_general(a, b, (dims, ((), ())), preferred_element_type=F32)


def project_kernel(u_ref, x_ref, keep_ref, send_ref):
    u_hi, u_lo = split(u_ref[...])
    x_hi, x_lo = split(x_ref[0])
    out = dot(
        jnp.concatenate([u_hi, u_hi, u_lo], axis=1),
        jnp.concatenate([x_hi, x_lo, x_hi], axis=0),
        ((1,), (0,)),
    )
    half = keep_ref.shape[1]
    keep_ref[0] = out[:half]
    send_ref[0] = out[half:]


def project(field, basis):
    slices, rows, cols = field.shape
    rank = basis.shape[0]
    out = jax.ShapeDtypeStruct((slices, rank // 2, cols), F32)
    block = pl.BlockSpec((1, rank // 2, cols), lambda s: (s, 0, 0))
    return pl.pallas_call(
        project_kernel,
        grid=(slices,),
        in_specs=[
            pl.BlockSpec((rank, rows), lambda s: (0, 0)),
            pl.BlockSpec((1, rows, cols), lambda s: (s, 0, 0)),
        ],
        out_specs=[block, block],
        out_shape=[out, out],
        compiler_params=pltpu.CompilerParams(vmem_limit_bytes=LIMIT),
        cost_estimate=pl.CostEstimate(
            flops=6 * slices * rows * cols * rank,
            bytes_accessed=4 * slices * cols * (rows + rank),
            transcendentals=0,
        ),
    )(basis, field)


def same_half_kernel(parts, x_ref, field_ref, out_ref, other_ref, a_ref, b_ref, send_sem, recv_sem):
    rows, cols = x_ref.shape[1:]
    b = rows // parts
    wide = out_ref.shape[2]
    half = other_ref.shape[0]
    gx = lax.axis_index("gx")
    step = pl.program_id(0)
    copy = pltpu.make_async_remote_copy(
        src_ref=field_ref.at[pl.ds((1 - gx) * half, half)],
        dst_ref=other_ref,
        send_sem=send_sem,
        recv_sem=recv_sem,
        device_id={"gx": 1 - gx},
        device_id_type=MESH,
    )

    @pl.when(step == 0)
    def _():
        barrier = pltpu.get_barrier_semaphore()
        pl.semaphore_signal(barrier, inc=1, device_id={"gx": 1 - gx}, device_id_type=MESH)
        pl.semaphore_wait(barrier, 1)
        copy.start()
        out_ref[...] = jnp.zeros_like(out_ref)

    hi, lo = split(x_ref[0])
    for n, v in enumerate((hi, hi, lo)):
        a_ref[:, n * cols : (n + 1) * cols] = v
    for n, v in enumerate((hi, lo, hi)):
        b_ref[:rows, n * cols : (n + 1) * cols] = v
        b_ref[rows:, n * cols : (n + 1) * cols] = v[: b_ref.shape[0] - rows]
    for i in range(parts):
        out_ref[i] += dot(a_ref[i * b : (i + 1) * b], b_ref[i * b : i * b + wide], ((1,), (1,)))

    @pl.when(step == pl.num_programs(0) - 1)
    def _():
        copy.wait()


def same_half(field, parts):
    slices, rows, cols = field.shape
    b = rows // parts
    wide = b * (parts // 2 + 1)
    return pl.pallas_call(
        functools.partial(same_half_kernel, parts),
        grid=(slices,),
        in_specs=[
            pl.BlockSpec((1, rows, cols), lambda s: (s, 0, 0)),
            pl.BlockSpec(memory_space=pl.ANY),
        ],
        out_specs=[
            pl.BlockSpec((parts, b, wide), lambda s: (0, 0, 0)),
            pl.BlockSpec(memory_space=pl.ANY),
        ],
        out_shape=[
            jax.ShapeDtypeStruct((parts, b, wide), F32),
            jax.ShapeDtypeStruct((slices // 2, rows, cols), F32),
        ],
        scratch_shapes=[
            pltpu.VMEM((rows, 3 * cols), BF16),
            pltpu.VMEM((rows + wide - b, 3 * cols), BF16),
            pltpu.SemaphoreType.DMA,
            pltpu.SemaphoreType.DMA,
        ],
        compiler_params=pltpu.CompilerParams(
            collective_id=2, has_side_effects=True, vmem_limit_bytes=LIMIT
        ),
        cost_estimate=pl.CostEstimate(
            flops=6 * slices * rows * cols * wide,
            bytes_accessed=4 * slices * cols * rows,
            transcendentals=0,
        ),
    )(field, field)


def cross_kernel(gx_ref, own_ref, other_ref, keep_ref, send_ref, a_ref, b_ref):
    rows, cols = own_ref.shape[1:]

    @pl.when(pl.program_id(0) == 0)
    def _():
        keep_ref[...] = jnp.zeros_like(keep_ref)
        send_ref[...] = jnp.zeros_like(send_ref)

    first = gx_ref[0] == 0
    own, other = own_ref[0], other_ref[0]
    hi, lo = split(jnp.where(first, own, other))
    for n, v in enumerate((hi, hi, lo)):
        a_ref[:, n * cols : (n + 1) * cols] = v
    hi, lo = split(jnp.where(first, other, own))
    for n, v in enumerate((hi, lo, hi)):
        b_ref[:, n * cols : (n + 1) * cols] = v
    parts, b, half = keep_ref.shape
    for ref, g in ((keep_ref, gx_ref[0]), (send_ref, 1 - gx_ref[0])):
        right = b_ref[pl.ds(pl.multiple_of(g * half, half), half)]
        for i in range(parts):
            ref[i] += dot(a_ref[i * b : (i + 1) * b], right, ((1,), (1,)))


def cross(gx, field, other, parts):
    slices, rows, cols = other.shape
    shape = (parts, rows // parts, rows // 2)
    return pl.pallas_call(
        cross_kernel,
        grid_spec=pltpu.PrefetchScalarGridSpec(
            num_scalar_prefetch=1,
            grid=(slices,),
            in_specs=[
                pl.BlockSpec((1, rows, cols), lambda s, g: (g[0] * slices + s, 0, 0)),
                pl.BlockSpec((1, rows, cols), lambda s, g: (s, 0, 0)),
            ],
            out_specs=[pl.BlockSpec(shape, lambda s, g: (0, 0, 0))] * 2,
            scratch_shapes=[pltpu.VMEM((rows, 3 * cols), BF16)] * 2,
        ),
        out_shape=[jax.ShapeDtypeStruct(shape, F32)] * 2,
        compiler_params=pltpu.CompilerParams(vmem_limit_bytes=LIMIT),
        cost_estimate=pl.CostEstimate(
            flops=6 * slices * rows * cols * rows,
            bytes_accessed=8 * slices * cols * rows,
            transcendentals=0,
        ),
    )(jnp.reshape(gx, (1,)).astype(jnp.int32), field, other)


def gram_y_kernel(gx_ref, y_ref, keep_ref, send_ref, b_ref):
    parts, depth, cols = y_ref.shape
    wide = keep_ref.shape[2]
    i = pl.program_id(0)

    @pl.when(i == 0)
    def _():
        for j in range(b_ref.shape[1] // cols):
            hi, lo = split(y_ref[j % parts])
            b_ref[:, j * cols : (j + 1) * cols] = jnp.concatenate([hi, lo, hi], axis=0)

    hi, lo = split(jnp.transpose(y_ref[i]))
    a = jnp.concatenate([hi, hi, lo], axis=1)
    start = pl.multiple_of(i * cols, cols)
    out = dot(a, b_ref[:, pl.ds(start, wide)], ((1,), (0,)))

    @pl.when(gx_ref[0] == 0)
    def _():
        keep_ref[0] = out[: cols // 2]
        send_ref[0] = out[cols // 2 :]

    @pl.when(gx_ref[0] == 1)
    def _():
        keep_ref[0] = out[cols // 2 :]
        send_ref[0] = out[: cols // 2]


def gram_y_terms(gx, y):
    parts, depth, cols = y.shape
    wide = cols * (parts // 2 + 1)
    return pl.pallas_call(
        gram_y_kernel,
        grid_spec=pltpu.PrefetchScalarGridSpec(
            num_scalar_prefetch=1,
            grid=(parts,),
            in_specs=[pl.BlockSpec((parts, depth, cols), lambda i, g: (0, 0, 0))],
            out_specs=[pl.BlockSpec((1, cols // 2, wide), lambda i, g: (i, 0, 0))] * 2,
            scratch_shapes=[pltpu.VMEM((3 * depth, parts * cols + wide - cols), BF16)],
        ),
        out_shape=[jax.ShapeDtypeStruct((parts, cols // 2, wide), F32)] * 2,
        compiler_params=pltpu.CompilerParams(vmem_limit_bytes=LIMIT),
        cost_estimate=pl.CostEstimate(
            flops=6 * parts * depth * cols * wide,
            bytes_accessed=4 * parts * cols * (wide + depth),
            transcendentals=0,
        ),
    )(jnp.reshape(gx, (1,)).astype(jnp.int32), y)


def spread(m, bits):
    return sum(((m >> (len(bits) - 1 - j)) & 1) << k for j, k in enumerate(bits))


def reduce_kernel(parts, planes, pieces, *refs):
    n = len(pieces)
    given = [a for a in range(n) if pieces[a][2]]
    g = len(given)
    ins, sends, outs, refs = refs[:n], refs[n : n + g], refs[n + g : 2 * n + g], refs[2 * n + g :]
    sends, partner = dict(zip(given, sends)), dict(zip(given, refs[:g]))
    refs = refs[g:]
    nbits = parts.bit_length() - 1
    steps = [refs[t * n : (t + 1) * n] for t in range(nbits)]
    z_in, z_mid, z_out = (refs[t * n : (t + 1) * n] for t in range(nbits, nbits + 3))
    send_sem, recv_sem = refs[(nbits + 3) * n :]
    gx, gy, gz = lax.axis_index("gx"), lax.axis_index("gy"), lax.axis_index("gz")
    terms = [partner.get(a, ins[a]) for a in range(n)]
    bit = [(gy // 2**k) % 2 for k in range(nbits)]
    side = gz // (planes // 2)
    depth = gz + side * (planes - 1 - 2 * gz)
    inward, outward = gz + 1 - 2 * side, gz - 1 + 2 * side
    middle = planes // 2 - 1

    chunks = []
    for a, (h, count, _) in enumerate(pieces):
        for c in range(count):
            rows = pl.ds(c * (h // count), h // count)
            order = list(range(nbits)) if c % 2 else list(range(nbits))[::-1]
            chunks.append((a, rows, order))

    barrier = pltpu.get_barrier_semaphore()
    for k in range(nbits):
        pl.semaphore_signal(
            barrier, inc=1, device_id={"gy": gy + (1 - 2 * bit[k]) * 2**k}, device_id_type=MESH
        )
    pl.semaphore_signal(barrier, inc=1, device_id={"gx": 1 - gx}, device_id_type=MESH)
    pl.semaphore_signal(barrier, inc=1, device_id={"gz": inward}, device_id_type=MESH)

    @pl.when(depth > 0)
    def _():
        pl.semaphore_signal(barrier, inc=1, device_id={"gz": outward}, device_id_type=MESH)

    pl.semaphore_wait(barrier, nbits + 2 + (depth + planes - 1) // planes)

    def across(c):
        a, rows, order = chunks[c]
        slot = parts // 2 + nbits + 2
        return pltpu.make_async_remote_copy(
            src_ref=sends[a].at[:, rows],
            dst_ref=partner[a].at[:, rows],
            send_sem=send_sem.at[c, slot],
            recv_sem=recv_sem.at[c, slot],
            device_id={"gx": 1 - gx},
            device_id_type=MESH,
        )

    def first(c):
        a, rows, order = chunks[c]
        if a in given:
            across(c).wait_recv()
            for m in range(parts):
                partner[a][m, rows] += ins[a][m, rows]
        for copy in halving(0, c):
            copy.start()

    def halving(t, c):
        a, rows, order = chunks[c]
        k = order[t]
        to = {"gy": gy + (1 - 2 * bit[k]) * 2**k}
        left = 2 ** (nbits - 1 - t)
        if t == 0:
            base = (1 - bit[k]) * 2**k
            return [
                pltpu.make_async_remote_copy(
                    src_ref=terms[a].at[base + spread(m, order[1:]), rows],
                    dst_ref=steps[0][a].at[m, rows],
                    send_sem=send_sem.at[c, m],
                    recv_sem=recv_sem.at[c, m],
                    device_id=to,
                    device_id_type=MESH,
                )
                for m in range(left)
            ]
        slot = parts // 2 + t - 1
        return [
            pltpu.make_async_remote_copy(
                src_ref=steps[t - 1][a].at[pl.ds((1 - bit[k]) * left, left), rows],
                dst_ref=steps[t][a].at[:, rows],
                send_sem=send_sem.at[c, slot],
                recv_sem=recv_sem.at[c, slot],
                device_id=to,
                device_id_type=MESH,
            )
        ]

    def along_z(c, kind):
        a, rows, order = chunks[c]
        slot = parts // 2 + nbits - 1 + kind
        total = steps[nbits - 1][a].at[0, rows]
        src = (total, total, z_out[a].at[rows])[kind]
        dst = (z_in, z_mid, z_out)[kind][a].at[rows]
        return pltpu.make_async_remote_copy(
            src_ref=src,
            dst_ref=dst,
            send_sem=send_sem.at[c, slot],
            recv_sem=recv_sem.at[c, slot],
            device_id={"gz": outward if kind == 2 else inward},
            device_id_type=MESH,
        )

    def stage(t, c):
        a, rows, order = chunks[c]
        if t < nbits:
            for copy in halving(t, c):
                copy.wait_recv()
            k = order[t]
            left = 2 ** (nbits - 1 - t)
            for m in range(left):
                if t == 0:
                    own = terms[a][bit[k] * 2**k + spread(m, order[1:]), rows]
                else:
                    own = steps[t - 1][a][bit[k] * left + m, rows]
                steps[t][a][m, rows] += own
            if t + 1 < nbits:
                for copy in halving(t + 1, c):
                    copy.start()
            else:
                @pl.when((depth == 0) if middle > 0 else (depth > planes))
                def _():
                    along_z(c, 0).start()

        elif t == nbits:
            @pl.when(depth > 0)
            def _():
                along_z(c, 0).wait_recv()
                steps[nbits - 1][a][0, rows] += z_in[a][rows]

            @pl.when(depth == middle)
            def _():
                along_z(c, 1).start()

            if middle > 1:
                @pl.when((depth > 0) & (depth < middle))
                def _():
                    along_z(c, 0).start()

        else:
            @pl.when(depth == middle)
            def _():
                along_z(c, 1).wait_recv()
                z_out[a][rows] = steps[nbits - 1][a][0, rows] + z_mid[a][rows]

            @pl.when(depth < middle)
            def _():
                along_z(c, 2).wait_recv()

            @pl.when(depth > 0)
            def _():
                along_z(c, 2).start()

            outs[a][rows] = z_out[a][rows]

    for c in range(len(chunks)):
        if chunks[c][0] in given:
            across(c).start()
    ahead = min(6, len(chunks))
    behind = list(range(nbits)) + [nbits + 1, nbits + 3]
    for c in range(ahead):
        first(c)
    for tick in range(len(chunks) + behind[-1]):
        if tick + ahead < len(chunks):
            first(tick + ahead)
        for t, late in enumerate(behind):
            if 0 <= tick - late < len(chunks):
                stage(t, tick - late)
    for c in range(len(chunks)):
        if chunks[c][0] in given:
            across(c).wait_send()
        for t in range(nbits):
            for copy in halving(t, c):
                copy.wait_send()

        @pl.when(depth < middle)
        def _():
            along_z(c, 0).wait_send()

        @pl.when(depth == middle)
        def _():
            along_z(c, 1).wait_send()

        @pl.when(depth > 0)
        def _():
            along_z(c, 2).wait_send()


def reduce_all(arrays, sends, parts, planes, counts, collective_id):
    pieces = [(x.shape[1], n, y is not None) for x, y, n in zip(arrays, sends, counts)]
    sends = [y for y in sends if y is not None]
    size = sum(x.size for x in arrays)
    nbits = parts.bit_length() - 1
    slots = parts // 2 + nbits + 3
    sems = pltpu.SemaphoreType.DMA((sum(counts), slots))
    vmem = pl.BlockSpec(memory_space=pltpu.VMEM)
    return pl.pallas_call(
        functools.partial(reduce_kernel, parts, planes, pieces),
        in_specs=[vmem] * len(arrays) + [pl.BlockSpec(memory_space=pl.ANY)] * len(sends),
        out_specs=[vmem] * len(arrays),
        out_shape=[jax.ShapeDtypeStruct(x.shape[1:], F32) for x in arrays],
        scratch_shapes=[pltpu.VMEM(x.shape, F32) for x in sends]
        + [
            pltpu.VMEM((parts // 2 ** (t + 1),) + x.shape[1:], F32) for t in range(nbits) for x in arrays
        ]
        + [pltpu.VMEM(x.shape[1:], F32) for x in arrays] * 3
        + [sems, sems],
        compiler_params=pltpu.CompilerParams(
            collective_id=collective_id, has_side_effects=True, vmem_limit_bytes=58 * 2**20
        ),
        cost_estimate=pl.CostEstimate(
            flops=2 * size, bytes_accessed=4 * size, transcendentals=0
        ),
    )(*arrays, *sends)


def swap(x, axis_name):
    return lax.ppermute(x, axis_name, [(0, 1), (1, 0)])


def mirror(block, step, parts):
    perm = [(i, (i + step) % parts) for i in range(parts)]
    return lax.ppermute(block, "gy", perm).T


def unroll(piece, gy, parts):
    b = piece.shape[1] // (parts // 2 + 1)
    blocks = [piece[:, k * b : (k + 1) * b] for k in range(parts // 2 + 1)]
    mirrored = [mirror(blocks[step], step, parts) for step in range(parts // 2 - 1, 0, -1)]
    return pick(blocks + mirrored, [(j + parts - gy) % parts for j in range(parts)])


def pick(blocks, places):
    stack = jnp.stack(blocks)
    return jnp.concatenate(
        [lax.dynamic_index_in_dim(stack, k, axis=0, keepdims=False) for k in places], axis=1
    )


def per_device(field, x_basis, y_basis):
    gx, gy = lax.axis_index("gx"), lax.axis_index("gy")
    parts, planes = lax.axis_size("gy"), lax.axis_size("gz")
    slices, rows, cols = field.shape
    rank = x_basis.shape[1]
    total_y, total_slices = cols * parts, slices * planes
    half = slices // 2

    basis = jnp.roll(x_basis.T, -gx * (rank // 2), axis=0)
    keep, send = project(field, basis)
    reduced = keep + swap(send, "gx")

    share = slices * (rank // 2) // parts
    y_basis_all = lax.all_gather(y_basis, "gy", axis=0)

    reduced, field = lax.optimization_barrier((reduced, field))
    y_rows = lax.all_to_all(reduced.reshape(parts, share, cols), "gy", 0, 0, tiled=True)
    same, other = same_half(field, parts)
    keep_x, send_x = cross(gx, field, other, parts)
    y_rows, same = lax.optimization_barrier((y_rows, same))
    keep_y, send_y = gram_y_terms(gx, y_rows)

    same, across, part_y = reduce_all(
        (same, keep_x, keep_y), (None, send_x, send_y), parts, planes, (4, 4, 4), 1
    )
    same, across = same / (total_y * total_slices), across / (total_y * total_slices)
    part_y = part_y / (rank * total_slices)

    core = jnp.einsum("gkl,glq->kq", y_rows, y_basis_all, precision=lax.Precision.HIGH)
    q = core.shape[1]
    core = lax.all_to_all(
        core.reshape(share, parts, q // parts).transpose(1, 0, 2), "gy", 0, 0, tiled=True
    )
    core = core.reshape(slices, rank // 2, q // parts).transpose(1, 0, 2)

    b = rows // parts
    diagonal = unroll(same, gy, parts)
    mine = across
    theirs = swap(mine, "gx")
    strip = jnp.where(
        gx == 0,
        jnp.concatenate([mine, theirs], axis=1),
        jnp.concatenate([theirs, mine], axis=1),
    )
    columns = lax.all_to_all(
        strip.reshape(b, parts, b).transpose(1, 2, 0), "gy", 0, 0, tiled=True
    )
    columns = columns.transpose(1, 0, 2).reshape(b, rows)
    gram_x = jnp.where(
        gx == 0,
        jnp.concatenate([diagonal, strip], axis=1),
        jnp.concatenate([columns, diagonal], axis=1),
    )

    blocks = [part_y[:, k * cols : (k + 1) * cols] for k in range(parts // 2 + 1)]
    mirrored = [mirror(blocks[step], step, parts) for step in range(parts // 2 - 1, 0, -1)]
    theirs = swap((part_y, mirrored), "gx")
    whole = jnp.where(
        gx == 0,
        jnp.concatenate([part_y, theirs[0]], axis=0),
        jnp.concatenate([theirs[0], part_y], axis=0),
    )
    blocks = [whole[:, k * cols : (k + 1) * cols] for k in range(parts // 2 + 1)]
    for own, got in zip(mirrored, theirs[1]):
        blocks.append(
            jnp.where(
                gx == 0,
                jnp.concatenate([own, got], axis=1),
                jnp.concatenate([got, own], axis=1),
            )
        )
    first = gx * (parts // 2) + parts - gy
    gram_y = pick(blocks, [(first + j) % parts for j in range(parts // 2)])
    return (gram_x, gram_y, core)


def solution(mesh):
    in_specs = (P("gz", "gx", "gy"), P("gx", None), P("gy", None))
    out_specs = (P(("gx", "gy"), None), P("gy", "gx"), P("gx", "gz", "gy"))
    return jax.shard_map(
        per_device, mesh=mesh, in_specs=in_specs, out_specs=out_specs, check_vma=False
    )
```
